32 devices in a mesh: clu: 16 (over z, y, x), rep: 2 (over core).
Axes of the slice: x: 2, y: 2, z: 4, core: 2. Of those that a mesh axis runs over, the one named last changes fastest.
Arguments:
- current: float32 [32, 2, 2, 2048], P('clu', None, 'rep'), may hold values from -6 to 6
- factors: float32 [64, 2, 2, 128, 2048], P(('clu', 'rep')), may hold values from -0.0625 to 0.0625
- ranks: int32 [64], P(('clu', 'rep')), may hold values from 8 to 40
- pair_clusters: int32 [64, 2], replicated, may hold values from 0 to 31, as said below
Outputs:
- field: float32 [32, 2, 2, 2048], P('clu', None, 'rep')
The draws below stay inside these ranges and needn't reach their ends.
Inputs may be any that keep to these rules, and one draw needn't show every extreme that they name: `pair_clusters`: the 4 cluster ids of the pairs of one device (pairs in blocks of 2 in order) are all different.
All inputs are finite; a program needn't handle non-finite values.
Results may differ from the reference program's by a relative error of at most 0.0003.
Values sent between devices are 32-bit elements; how exact they have to be, the bound alone decides.
No kernel may reach another device: no remote copies, remote signals or barrier semaphores. Data moves between devices by JAX's collectives and lax.ppermute only.
A program may use at most 128 MiB of HBM per device.

```python
import jax
import jax.numpy as jnp
from jax import lax

CS = 2048
RPAD = 128
NRHS = 2
PAIR_DEV = 2
NCLU = 32
PAIRS = 64


def draw_pair_clusters(key, part):
    blocks = PAIRS // PAIR_DEV
    end_count = 2 * PAIR_DEV

    def draw_block(block_key):
        order = jax.random.permutation(block_key, NCLU)
        return order[:end_count].astype(jnp.int32)
    block_keys = jax.vmap(lambda block: jax.random.fold_in(key, block))(jnp.arange(blocks, dtype=jnp.int32))
    return jax.vmap(draw_block)(block_keys).reshape(PAIRS, 2).astype(jnp.int32)


def place_ends(drawn, rng, least, largest):
    longest = drawn.shape.index(max(drawn.shape))
    spots = []
    for shift in (0, 1):
        where = [jax.random.randint(jax.random.fold_in(rng, axis), (), 0, length) for axis, length in enumerate(drawn.shape)]
        where[longest] = (where[longest] + shift) % drawn.shape[longest]
        spots.append(tuple(where))
    return drawn.at[spots[0]].set(least).at[spots[1]].set(largest)


def shard_levels(stream_key, extent, cuts, smallest, top_value):
    level, own = 1.0, jax.random.fold_in(stream_key, 6)
    for dim, shards_of in cuts:
        draws = jnp.exp(jax.random.uniform(jax.random.fold_in(own, dim), (shards_of,), jnp.float32, smallest / len(cuts), top_value / len(cuts)))
        level = level * jnp.repeat(draws, extent[dim] // shards_of).reshape([-1 if axis == dim else 1 for axis in range(len(extent))])
    return level


def centred(key, extent, scale, reach, pieces=(), held_as=jnp.bfloat16):
    drawn = scale * jax.random.normal(key, extent, jnp.float32)
    if pieces:
        drawn = drawn * shard_levels(key, extent, pieces, -0.22, 0.18)
    return jnp.clip(drawn, -reach, reach).astype(held_as)


def setup_inputs(seed: int = 0) -> dict:
    key_of = jax.random.split(jax.random.key(seed), 5)
    return {
        "current": centred(key_of[0], (NCLU, 2, NRHS, CS), 1.0, 6.0, ((0, 16), (2, 2)), jnp.float32),
        "factors": centred(key_of[1], (PAIRS, 2, 2, RPAD, CS), (4 * CS) ** -0.5, 0.0625, ((0, 32),), jnp.float32),
        "ranks": place_ends(jax.random.randint(key_of[2], (PAIRS,), RPAD // 16, RPAD * 5 // 16 + 1), jax.random.fold_in(key_of[2], 1), RPAD // 16, (RPAD * 5 // 16 + 1) - 1).astype(jnp.int32),
        "pair_clusters": draw_pair_clusters(jax.random.fold_in(key_of[4], 71), 0),
    }


def project_rows(factor, vector, rank_mask):
    high = lax.Precision.HIGHEST
    real_part = jnp.einsum('prc,pkc->prk', factor[:, 0], vector[:, 0], precision=high) - jnp.einsum('prc,pkc->prk', factor[:, 1], vector[:, 1], precision=high)
    imag_part = jnp.einsum('prc,pkc->prk', factor[:, 0], vector[:, 1], precision=high) + jnp.einsum('prc,pkc->prk', factor[:, 1], vector[:, 0], precision=high)
    return jnp.stack((real_part, imag_part), axis=1) * rank_mask[:, None, :, None]


def expand_rows(factor, projected):
    high = lax.Precision.HIGHEST
    real_part = jnp.einsum('prc,prk->pkc', factor[:, 0], projected[:, 0], precision=high) - jnp.einsum('prc,prk->pkc', factor[:, 1], projected[:, 1], precision=high)
    imag_part = jnp.einsum('prc,prk->pkc', factor[:, 0], projected[:, 1], precision=high) + jnp.einsum('prc,prk->pkc', factor[:, 1], projected[:, 0], precision=high)
    return jnp.stack((real_part, imag_part), axis=1)


def pair_terms(factor_block, rank_list, row_current, col_current):
    left_factor = factor_block[:, 0]
    right_factor = factor_block[:, 1]
    rank_mask = (jnp.arange(factor_block.shape[3], dtype=jnp.int32)[None, :] < rank_list[:, None]).astype(factor_block.dtype)
    row_terms = expand_rows(left_factor, project_rows(right_factor, col_current, rank_mask))
    col_terms = expand_rows(right_factor, project_rows(left_factor, row_current, rank_mask))
    return row_terms, col_terms


def reference(current, factors, ranks, pair_clusters):
    blocks = PAIRS // PAIR_DEV
    result_field = jnp.zeros_like(current)

    def accumulate(result_field, block):
        offset_rows = (block * PAIR_DEV).astype(jnp.int32)
        factor_block = lax.dynamic_slice_in_dim(factors, offset_rows, PAIR_DEV, 0)
        rank_list = lax.dynamic_slice_in_dim(ranks, offset_rows, PAIR_DEV, 0)
        cluster_ids = lax.dynamic_slice_in_dim(pair_clusters, offset_rows, PAIR_DEV, 0)
        row_terms, col_terms = pair_terms(factor_block, rank_list, current[cluster_ids[:, 0]], current[cluster_ids[:, 1]])
        result_field = result_field.at[cluster_ids[:, 0]].add(row_terms)
        result_field = result_field.at[cluster_ids[:, 1]].add(col_terms)
        return result_field, None

    result_field, _ = lax.scan(accumulate, result_field, jnp.arange(blocks, dtype=jnp.int32))
    return result_field
```

```python
import jax
import jax.numpy as jnp
from jax import lax
from jax.experimental import pallas as pl
from jax.experimental.pallas import tpu as pltpu
from jax.sharding import PartitionSpec as P

MAX_RANK = 40
LANES = 128


def pair_kernel(n_rep, pair_count, ids_ref, cur_ref, own_ref, peer_ref, out_ref):
    chunks = cur_ref.shape[1] // 2
    block = lax.axis_index("clu") * n_rep + lax.axis_index("rep")
    other = lax.axis_index("clu") * n_rep + (n_rep - 1 - lax.axis_index("rep"))
    out_ref[...] = jnp.zeros_like(out_ref)
    for which, ref in ((block, own_ref), (other, peer_ref)):
        for p in range(pair_count):
            row = ids_ref[which * pair_count + p, 0]
            col = ids_ref[which * pair_count + p, 1]
            for src, dst, proj, expand in ((col, row, 1, 0), (row, col, 0, 1)):
                acc_re = jnp.zeros((MAX_RANK, LANES), jnp.float32)
                acc_im = jnp.zeros((MAX_RANK, LANES), jnp.float32)
                for c in range(chunks):
                    f_re = ref[p, proj, 0, :, c * LANES : (c + 1) * LANES]
                    f_im = ref[p, proj, 1, :, c * LANES : (c + 1) * LANES]
                    z_re = cur_ref[src, c : c + 1, :]
                    z_im = cur_ref[src, chunks + c : chunks + c + 1, :]
                    acc_re = acc_re + f_re * z_re - f_im * z_im
                    acc_im = acc_im + f_re * z_im + f_im * z_re
                t_re = jnp.sum(acc_re, axis=1, keepdims=True)
                t_im = jnp.sum(acc_im, axis=1, keepdims=True)
                for c in range(chunks):
                    f_re = ref[p, expand, 0, :, c * LANES : (c + 1) * LANES]
                    f_im = ref[p, expand, 1, :, c * LANES : (c + 1) * LANES]
                    g_re = jnp.sum(f_re * t_re - f_im * t_im, axis=0, keepdims=True)
                    g_im = jnp.sum(f_re * t_im + f_im * t_re, axis=0, keepdims=True)
                    out_ref[dst, c : c + 1, :] += g_re
                    out_ref[dst, chunks + c : chunks + c + 1, :] += g_im


def local(current, factors, ranks, pair_clusters):
    clu_count, _, _, unknowns = current.shape
    pair_count = factors.shape[0]
    n_clu = lax.axis_size("clu")
    n_rep = lax.axis_size("rep")
    chunks = unknowns // LANES
    rows = clu_count * 2 * chunks
    mine = current.reshape(rows, LANES)
    spread = jnp.broadcast_to(mine[None], (n_clu, rows, LANES))
    gathered = lax.all_to_all(spread, "clu", 0, 0)
    gathered = gathered.reshape(n_clu * clu_count, 2 * chunks, LANES)
    mask = jnp.arange(MAX_RANK, dtype=jnp.int32)[None, :] < ranks[:, None]
    own = jnp.where(mask[:, None, None, :, None], factors[:, :, :, :MAX_RANK, :], 0.0)
    peer = lax.ppermute(own, "rep", [(r, n_rep - 1 - r) for r in range(n_rep)])
    vmem = pl.BlockSpec(memory_space=pltpu.VMEM)
    placed = pl.pallas_call(
        lambda *refs: pair_kernel(n_rep, pair_count, *refs),
        out_shape=jax.ShapeDtypeStruct((n_clu * clu_count, 2 * chunks, LANES), jnp.float32),
        in_specs=[pl.BlockSpec(memory_space=pltpu.SMEM), vmem, vmem, vmem],
        out_specs=vmem,
        compiler_params=pltpu.CompilerParams(vmem_limit_bytes=32 * 1024 * 1024),
    )(pair_clusters, gathered, own, peer)
    back = lax.all_to_all(placed.reshape(n_clu, rows, LANES), "clu", 0, 0)
    return jnp.sum(back, axis=0).reshape(current.shape)


def solution(mesh):
    placed = (
        P("clu", None, "rep", None),
        P(("clu", "rep"), None, None, None, None),
        P(("clu", "rep")),
        P(),
    )
    return jax.shard_map(
        local, mesh=mesh, in_specs=placed, out_specs=P("clu", None, "rep", None), check_vma=False
    )
```

```python
import jax
import jax.numpy as jnp
from jax import lax
from jax.experimental import pallas as pl
from jax.experimental.pallas import tpu as pltpu
from jax.sharding import PartitionSpec as P

MAX_RANK = 40
LANES = 128


def inner_size(n_clu):
    inner = 1
    while inner * inner * 4 <= n_clu and n_clu % (2 * inner) == 0:
        inner *= 2
    return inner


def partner(index, step, size):
    if size & (size - 1) == 0:
        return index ^ step
    return (step - index) % size


def slot_of(index, me, size):
    if size & (size - 1) == 0:
        return index ^ me
    return lax.rem(index + me, size)


def swap(array, step, stride, size, n_clu):
    pairs = []
    for i in range(n_clu):
        digit = (i // stride) % size
        pairs.append((i, i + (partner(digit, step, size) - digit) * stride))
    return lax.ppermute(array, "clu", pairs)


def pair_kernel(n_rep, pair_count, clu_count, inner, outer, *refs):
    ids_ref = refs[0]
    cur_refs = refs[1 : 1 + inner]
    own_ref, peer_ref = refs[1 + inner : 3 + inner]
    out_refs = refs[3 + inner : 3 + 2 * inner]
    z_ref, sum_ref = refs[3 + 2 * inner :]
    chunks = z_ref.shape[0] // 2
    clu = lax.axis_index("clu")
    rep = lax.axis_index("rep")
    mine, other = clu * n_rep + rep, clu * n_rep + (n_rep - 1 - rep)
    clu_in, clu_out = lax.rem(clu, inner), lax.div(clu, inner)

    def place(cluster):
        owner, part = lax.div(cluster, clu_count), lax.rem(cluster, clu_count)
        slot_in = slot_of(lax.rem(owner, inner), clu_in, inner)
        slot_out = slot_of(lax.div(owner, inner), clu_out, outer)
        return slot_in, slot_out * clu_count + part

    sum_ref[...] = jnp.zeros_like(sum_ref)
    for block, ref in ((mine, own_ref), (other, peer_ref)):
        for p in range(pair_count):
            row = place(ids_ref[block * pair_count + p, 0])
            col = place(ids_ref[block * pair_count + p, 1])
            for src, dst, proj, expand in ((col, row, 1, 0), (row, col, 0, 1)):
                z = cur_refs[0][src[1]]
                for s in range(1, inner):
                    z = jnp.where(src[0] == s, cur_refs[s][src[1]], z)
                z_ref[...] = z
                acc_re = jnp.zeros((MAX_RANK, LANES), jnp.float32)
                acc_im = jnp.zeros((MAX_RANK, LANES), jnp.float32)
                for c in range(chunks):
                    f_re = ref[p, proj, 0, :, c * LANES : (c + 1) * LANES]
                    f_im = ref[p, proj, 1, :, c * LANES : (c + 1) * LANES]
                    z_re = z_ref[c : c + 1, :]
                    z_im = z_ref[chunks + c : chunks + c + 1, :]
                    acc_re = acc_re + f_re * z_re - f_im * z_im
                    acc_im = acc_im + f_re * z_im + f_im * z_re
                t_re = jnp.sum(acc_re, axis=1, keepdims=True)
                t_im = jnp.sum(acc_im, axis=1, keepdims=True)
                for c in range(chunks):
                    f_re = ref[p, expand, 0, :, c * LANES : (c + 1) * LANES]
                    f_im = ref[p, expand, 1, :, c * LANES : (c + 1) * LANES]
                    g_re = jnp.sum(f_re * t_re - f_im * t_im, axis=0, keepdims=True)
                    g_im = jnp.sum(f_re * t_im + f_im * t_re, axis=0, keepdims=True)
                    sum_ref[dst[0], dst[1], c : c + 1, :] += g_re
                    sum_ref[dst[0], dst[1], chunks + c : chunks + c + 1, :] += g_im
    for s in range(inner):
        out_refs[s][...] = sum_ref[s]


def local(current, factors, ranks, pair_clusters):
    clu_count, _, _, unknowns = current.shape
    pair_count = factors.shape[0]
    n_clu = lax.axis_size("clu")
    n_rep = lax.axis_size("rep")
    inner = inner_size(n_clu)
    outer = n_clu // inner
    chunks = unknowns // LANES
    mine = current.reshape(clu_count, 2 * chunks, LANES)
    line = jnp.concatenate(
        [mine] + [swap(mine, s, inner, outer, n_clu) for s in range(1, outer)]
    )
    planes = [line] + [swap(line, s, 1, inner, n_clu) for s in range(1, inner)]
    mask = jnp.arange(MAX_RANK, dtype=jnp.int32)[None, :] < ranks[:, None]
    own = jnp.where(mask[:, None, None, :, None], factors[:, :, :, :MAX_RANK, :], 0.0)
    peer = lax.ppermute(own, "rep", [(r, n_rep - 1 - r) for r in range(n_rep)])
    vmem = pl.BlockSpec(memory_space=pltpu.VMEM)
    line_shape = (outer * clu_count, 2 * chunks, LANES)
    parts = pl.pallas_call(
        lambda *refs: pair_kernel(n_rep, pair_count, clu_count, inner, outer, *refs),
        out_shape=[jax.ShapeDtypeStruct(line_shape, jnp.float32)] * inner,
        in_specs=[pl.BlockSpec(memory_space=pltpu.SMEM)] + [vmem] * (inner + 2),
        out_specs=[vmem] * inner,
        scratch_shapes=[
            pltpu.VMEM((2 * chunks, LANES), jnp.float32),
            pltpu.VMEM((inner,) + line_shape, jnp.float32),
        ],
        compiler_params=pltpu.CompilerParams(vmem_limit_bytes=32 * 1024 * 1024),
    )(pair_clusters, *planes, own, peer)
    total = parts[0]
    for s in range(1, inner):
        total = total + swap(parts[s], s, 1, inner, n_clu)
    total = total.reshape(outer, clu_count, 2 * chunks, LANES)
    field = total[0]
    for s in range(1, outer):
        field = field + swap(total[s], s, inner, outer, n_clu)
    return field.reshape(current.shape)


def solution(mesh):
    placed = (
        P("clu", None, "rep", None),
        P(("clu", "rep"), None, None, None, None),
        P(("clu", "rep")),
        P(),
    )
    return jax.shard_map(
        local, mesh=mesh, in_specs=placed, out_specs=P("clu", None, "rep", None), check_vma=False
    )
```

```python
import jax
import jax.numpy as jnp
from jax import lax
from jax.experimental import pallas as pl
from jax.experimental.pallas import tpu as pltpu
from jax.sharding import PartitionSpec as P

MAX_RANK = 40
LANES = 128


def inner_size(n_clu):
    inner = 1
    while inner * inner * 4 <= n_clu and n_clu % (2 * inner) == 0:
        inner *= 2
    return inner


def partner(index, step, size):
    if size & (size - 1) == 0:
        return index ^ step
    return (step - index) % size


def slot_of(index, me, size):
    if size & (size - 1) == 0:
        return index ^ me
    return lax.rem(index + me, size)


def swap(array, step, stride, size, n_clu):
    pairs = []
    for i in range(n_clu):
        digit = (i // stride) % size
        pairs.append((i, i + (partner(digit, step, size) - digit) * stride))
    return lax.ppermute(array, "clu", pairs)


def pair_kernel(n_rep, pair_count, clu_count, inner, outer, *refs):
    ids_ref = refs[0]
    cur_refs = refs[1 : 1 + inner]
    own_ref, peer_ref = refs[1 + inner : 3 + inner]
    out_refs = refs[3 + inner : 3 + 2 * inner]
    sum_ref, z_ref, g_ref = refs[3 + 2 * inner :]
    chunks = z_ref.shape[1] // 2
    clu = lax.axis_index("clu")
    rep = lax.axis_index("rep")
    mine, other = clu * n_rep + rep, clu * n_rep + (n_rep - 1 - rep)
    clu_in, clu_out = lax.rem(clu, inner), lax.div(clu, inner)
    raw = [
        ids_ref[block * pair_count + p, e]
        for block in (mine, other)
        for p in range(pair_count)
        for e in (0, 1)
    ]
    def place(cluster):
        owner, part = lax.div(cluster, clu_count), lax.rem(cluster, clu_count)
        slot_in = slot_of(lax.rem(owner, inner), clu_in, inner)
        slot_out = slot_of(lax.div(owner, inner), clu_out, outer)
        slot_out = jnp.where(slot_out == 0, 0, outer - slot_out)
        return slot_in, slot_out * clu_count + part
    ends = [place(c) for c in raw]
    for s in range(inner):
        sum_ref[s] = jnp.zeros(sum_ref.shape[1:], jnp.float32)
    for k, (s_in, s_out) in enumerate(ends):
        z = cur_refs[0][s_out]
        for s in range(1, inner):
            z = jnp.where(s_in == s, cur_refs[s][s_out], z)
        z_ref[k] = z
    for k in range(len(ends)):
        ref = (own_ref, peer_ref)[k // (2 * pair_count)]
        p, e = (k // 2) % pair_count, k % 2
        src = k ^ 1
        acc_re = jnp.zeros((MAX_RANK, LANES), jnp.float32)
        acc_im = jnp.zeros((MAX_RANK, LANES), jnp.float32)
        for c in range(chunks):
            f_re = ref[p, 1 - e, 0, :, c * LANES : (c + 1) * LANES]
            f_im = ref[p, 1 - e, 1, :, c * LANES : (c + 1) * LANES]
            z_re = z_ref[src, c : c + 1, :]
            z_im = z_ref[src, chunks + c : chunks + c + 1, :]
            acc_re = acc_re + (f_re * z_re - f_im * z_im)
            acc_im = acc_im + (f_re * z_im + f_im * z_re)
        t_re = jnp.sum(acc_re, axis=1, keepdims=True)
        t_im = jnp.sum(acc_im, axis=1, keepdims=True)
        for c in range(chunks):
            f_re = ref[p, e, 0, :, c * LANES : (c + 1) * LANES]
            f_im = ref[p, e, 1, :, c * LANES : (c + 1) * LANES]
            g_ref[k, c : c + 1, :] = jnp.sum(f_re * t_re - f_im * t_im, axis=0, keepdims=True)
            g_ref[k, chunks + c : chunks + c + 1, :] = jnp.sum(f_re * t_im + f_im * t_re, axis=0, keepdims=True)
    for k, (s_in, s_out) in enumerate(ends):
        sum_ref[s_in, s_out] += g_ref[k]
    for s in range(inner):
        out_refs[s][...] = sum_ref[s]


def stage_kernel(src_ref, dst_ref, sems):
    copies = [
        pltpu.make_async_copy(src_ref.at[p, e, d], dst_ref.at[p, e, d], sems.at[p, e, d])
        for p in range(src_ref.shape[0])
        for e in (0, 1)
        for d in (0, 1)
    ]
    for copy in copies:
        copy.start()
    for copy in copies:
        copy.wait()


def staged(array):
    return pl.pallas_call(
        stage_kernel,
        out_shape=jax.ShapeDtypeStruct(array.shape, array.dtype),
        in_specs=[pl.BlockSpec(memory_space=pl.ANY)],
        out_specs=pl.BlockSpec(memory_space=pltpu.VMEM),
        scratch_shapes=[pltpu.SemaphoreType.DMA(array.shape[:3])],
        compiler_params=pltpu.CompilerParams(vmem_limit_bytes=8 * 1024 * 1024),
        cost_estimate=pl.CostEstimate(flops=0, bytes_accessed=8 * array.size, transcendentals=0),
    )(array)


def local(current, factors, ranks, pair_clusters):
    clu_count, _, _, unknowns = current.shape
    pair_count = factors.shape[0]
    n_clu = lax.axis_size("clu")
    n_rep = lax.axis_size("rep")
    inner = inner_size(n_clu)
    outer = n_clu // inner
    chunks = unknowns // LANES
    mine = current.reshape(clu_count, 2 * chunks, LANES)
    line = jnp.concatenate(
        [mine] + [swap(mine, s, inner, outer, n_clu) for s in reversed(range(1, outer))]
    )
    used = factors[:, :, :, :MAX_RANK, :]
    rank_row = lax.broadcasted_iota(jnp.int32, used.shape, 3)
    own = jnp.where(rank_row < ranks[:, None, None, None, None], used, 0.0)
    own, line = lax.optimization_barrier((own, line))
    planes = [line] + [swap(line, s, 1, inner, n_clu) for s in range(1, inner)]
    peer = lax.ppermute(own, "rep", [(r, n_rep - 1 - r) for r in range(n_rep)])
    peer = staged(peer)
    vmem = pl.BlockSpec(memory_space=pltpu.VMEM)
    line_shape = (outer * clu_count, 2 * chunks, LANES)
    parts = pl.pallas_call(
        lambda *refs: pair_kernel(n_rep, pair_count, clu_count, inner, outer, *refs),
        out_shape=[jax.ShapeDtypeStruct(line_shape, jnp.float32)] * inner,
        in_specs=[vmem] * (inner + 3),
        out_specs=[vmem] * inner,
        scratch_shapes=[
            pltpu.VMEM((inner,) + line_shape, jnp.float32),
            pltpu.VMEM((4 * pair_count, 2 * chunks, LANES), jnp.float32),
            pltpu.VMEM((4 * pair_count, 2 * chunks, LANES), jnp.float32),
        ],
        compiler_params=pltpu.CompilerParams(vmem_limit_bytes=8 * 1024 * 1024),
    )(pair_clusters, *planes, own, peer)
    total = parts[0]
    for s in reversed(range(1, inner)):
        total = total + swap(parts[s], s, 1, inner, n_clu)
    total = total.reshape(outer, clu_count, 2 * chunks, LANES)
    field = total[0]
    for s in range(1, outer):
        field = field + swap(total[outer - s], s, inner, outer, n_clu)
    return field.reshape(current.shape)


def solution(mesh):
    placed = (
        P("clu", None, "rep", None),
        P(("clu", "rep"), None, None, None, None),
        P(("clu", "rep")),
        P(),
    )
    return jax.shard_map(
        local, mesh=mesh, in_specs=placed, out_specs=P("clu", None, "rep", None), check_vma=False
    )
```
